128 devices in a mesh: col: 16 (over x, y), row: 8 (over z, core).
Axes of the slice: x: 4, y: 4, z: 4, core: 2. Of those that a mesh axis runs over, the one named last changes fastest.
Arguments:
- right_side: float32 [8, 128, 32, 128], P(None, ('col', 'row')), may hold values from -6 to 6
- lower_inverse: float32 [8, 128, 128, 128], P(None, ('col', 'row')), as said below
- lower_blocks: bfloat16 [7, 16, 8, 8, 4, 128, 128], P(None, 'col', None, 'row'), may hold values from -0.046875 to 0.046875
- lower_pattern: int32 [7, 16, 8, 8, 4], P(None, 'col', None, 'row'), may hold values from 0 to 111, as said below
- upper_inverse: float32 [8, 128, 128, 128], P(None, ('col', 'row')), as said below
- upper_blocks: bfloat16 [7, 16, 8, 8, 4, 128, 128], P(None, 'col', None, 'row'), may hold values from -0.046875 to 0.046875
- upper_pattern: int32 [7, 16, 8, 8, 4], P(None, 'col', None, 'row'), may hold values from 16 to 127, as said below
Outputs:
- forward_solution: float32 [8, 128, 32, 128], P(None, ('col', 'row'))
- solution: float32 [8, 128, 32, 128], P(None, ('col', 'row'))
The draws below stay inside these ranges and needn't reach their ends.
Inputs may be any that keep to these rules, and one draw needn't show every extreme that they name: `lower_pattern`: an L block of level i + 1 points at a supernode of levels 0 to i. `upper_pattern`: A U block of level i points at a supernode of levels i + 1 to 7. `lower_inverse`: lower triangular. `upper_inverse`: upper triangular.
All inputs are finite; a program needn't handle non-finite values.
Results may differ from the reference program's by a relative error of at most 0.003.
Values may be sent and summed in bfloat16 or wider, within the bound.
No kernel may reach another device: no remote copies, remote signals or barrier semaphores. Data moves between devices by JAX's collectives and lax.ppermute only.
A program may use at most 64 MiB of HBM per device.

```python
import math
import jax
import jax.numpy as jnp
from jax import lax

BLOCK = 128
RHS = 32
LEVELS = 8
SLOTS = 4
PER_LEVEL = 128
N_COL = 16
N_ROW = 8


def triangle_inverse(key, below, off_scale):
    key_diag, key_off = jax.random.split(key)
    shape = (LEVELS, PER_LEVEL, BLOCK, BLOCK)
    diagonal = jax.random.uniform(key_diag, (LEVELS, PER_LEVEL, BLOCK), jnp.float32, 0.7, 1.3)
    offdiag = jax.random.normal(key_off, shape, jnp.float32) * off_scale
    rows_idx = jnp.arange(BLOCK)[:, None]
    cols_idx = jnp.arange(BLOCK)[None, :]
    if below:
        keep = rows_idx > cols_idx
    else:
        keep = rows_idx < cols_idx
    eye_mask = (rows_idx == cols_idx).astype(jnp.float32)
    return jnp.where(keep, offdiag, 0.0) + eye_mask * diagonal[..., None]


def draw_lower_inverse(key, part):
    key = jax.random.fold_in(key, 11)
    return triangle_inverse(key, True, 0.5 / math.sqrt(BLOCK))


def draw_upper_inverse(key, part):
    key = jax.random.fold_in(key, 12)
    return triangle_inverse(key, False, 0.5 / math.sqrt(BLOCK))


def draw_lower_pattern(key, part):
    key = jax.random.fold_in(key, 13)
    shape = (LEVELS - 1, N_COL, N_ROW, N_ROW, SLOTS)
    raw_bits = jax.random.randint(key, shape, 0, 2 ** 30, jnp.int32)
    bound = (jnp.arange(LEVELS - 1, dtype=jnp.int32) + 1) * N_COL
    values = raw_bits % bound[:, None, None, None, None]
    values = values.at[LEVELS - 2, 0, 0, 0, 0].set((LEVELS - 1) * N_COL - 1)
    values = values.at[LEVELS - 2, 0, 0, 0, 1].set(0)
    return values


def draw_upper_pattern(key, part):
    key = jax.random.fold_in(key, 14)
    shape = (LEVELS - 1, N_COL, N_ROW, N_ROW, SLOTS)
    raw_bits = jax.random.randint(key, shape, 0, 2 ** 30, jnp.int32)
    lowest = (jnp.arange(LEVELS - 1, dtype=jnp.int32) + 1) * N_COL
    span = LEVELS * N_COL - lowest
    values = lowest[:, None, None, None, None] + raw_bits % span[:, None, None, None, None]
    values = values.at[0, 0, 0, 0, 0].set(LEVELS * N_COL - 1)
    values = values.at[0, 0, 0, 0, 1].set(N_COL)
    return values


def levels(stream_key, extent, shards, least, top_value):
    def one(position, blocks):
        steps = jax.random.uniform(jax.random.fold_in(jax.random.fold_in(stream_key, 6), position), (blocks,), jnp.float32, least / len(shards), top_value / len(shards))
        return jnp.repeat(jnp.exp(steps), extent[position] // blocks).reshape((-1,) + (1,) * (len(extent) - position - 1))

    gain = one(*shards[0])
    for cut in shards[1:]:
        gain = gain * one(*cut)
    return gain


def bell_draw(own_key, dims, spread, most, cuts=(), kind=jnp.bfloat16):
    entries = jax.random.normal(own_key, dims, jnp.float32) * spread
    if len(cuts) > 0:
        entries = levels(own_key, dims, cuts, -0.22, 0.18) * entries
    return jnp.clip(entries, min=-most, max=most).astype(kind)


def setup_inputs(seed: int = 0) -> dict:
    arg_keys = jax.random.split(jax.random.key(seed), 8)
    return {
        "right_side": bell_draw(arg_keys[0], (LEVELS, PER_LEVEL, RHS, BLOCK), 1.0, 6.0, ((1, 128),), jnp.float32),
        "lower_inverse": draw_lower_inverse(jax.random.fold_in(arg_keys[7], 71), 0),
        "lower_blocks": bell_draw(arg_keys[2], (LEVELS - 1, N_COL, N_ROW, N_ROW, SLOTS, BLOCK, BLOCK), (4 * BLOCK * N_ROW * SLOTS) ** -0.5, 0.046875, ((1, 16), (3, 8))),
        "lower_pattern": draw_lower_pattern(jax.random.fold_in(arg_keys[7], 71), 0),
        "upper_inverse": draw_upper_inverse(jax.random.fold_in(arg_keys[7], 71), 0),
        "upper_blocks": bell_draw(arg_keys[5], (LEVELS - 1, N_COL, N_ROW, N_ROW, SLOTS, BLOCK, BLOCK), (4 * BLOCK * N_ROW * SLOTS) ** -0.5, 0.046875, ((1, 16), (3, 8))),
        "upper_pattern": draw_upper_pattern(jax.random.fold_in(arg_keys[7], 71), 0),
    }


def level_terms(history, blocks, pattern):
    rows_index = jnp.arange(N_ROW, dtype=jnp.int32)[None, :, None]

    def one_column(pair):
        block_col, pattern_col = pair
        picked = history[rows_index, pattern_col]
        return jnp.einsum('mrsxj,mrsoj->mxo', picked.astype(jnp.float32), block_col.astype(jnp.float32))

    partial_value = lax.map(one_column, (blocks, pattern))
    return partial_value.reshape(PER_LEVEL, RHS, BLOCK)


def row_history(rounded):
    grid_form = rounded.reshape(LEVELS, N_COL, N_ROW, RHS, BLOCK)
    return jnp.transpose(grid_form, (2, 0, 1, 3, 4)).reshape(N_ROW, LEVELS * N_COL, RHS, BLOCK)


def apply_inverse(inverse, vectors):
    return jnp.einsum('qxi,qoi->qxo', vectors, inverse, precision=lax.Precision.HIGHEST)


def reference(right_side, lower_inverse, lower_blocks, lower_pattern, upper_inverse, upper_blocks, upper_pattern):
    forward = jnp.zeros((LEVELS, PER_LEVEL, RHS, BLOCK), jnp.float32)
    rounded = jnp.zeros((LEVELS, PER_LEVEL, RHS, BLOCK), jnp.bfloat16)
    for tier_index in range(LEVELS):
        residual_now = right_side[tier_index]
        if tier_index > 0:
            residual_now = residual_now - level_terms(row_history(rounded), lower_blocks[tier_index - 1], lower_pattern[tier_index - 1])
        solved = apply_inverse(lower_inverse[tier_index], residual_now)
        forward = forward.at[tier_index].set(solved)
        rounded = rounded.at[tier_index].set(solved.astype(jnp.bfloat16))
    solution = jnp.zeros((LEVELS, PER_LEVEL, RHS, BLOCK), jnp.float32)
    rounded = jnp.zeros((LEVELS, PER_LEVEL, RHS, BLOCK), jnp.bfloat16)
    for tier_index in range(LEVELS - 1, -1, -1):
        residual_now = forward[tier_index]
        if tier_index < LEVELS - 1:
            residual_now = residual_now - level_terms(row_history(rounded), upper_blocks[tier_index], upper_pattern[tier_index])
        solved = apply_inverse(upper_inverse[tier_index], residual_now)
        solution = solution.at[tier_index].set(solved)
        rounded = rounded.at[tier_index].set(solved.astype(jnp.bfloat16))
    return forward, solution
```

```python
import jax
import jax.numpy as jnp
from jax import lax
from jax.sharding import PartitionSpec as P


def apply_inverse(inverse, vectors):
    return jnp.einsum("xi,oi->xo", vectors, inverse, precision=lax.Precision.HIGHEST)


def level_terms(history, blocks, pattern):
    picked = history[pattern]
    return jnp.einsum("msxj,msoj->mxo", picked, blocks, preferred_element_type=jnp.float32)


def reduce_rows(partial_value):
    return lax.all_to_all(partial_value, "row", 0, 0, tiled=True).sum(axis=0)


def share_solved(solved):
    copies = jnp.broadcast_to(solved.astype(jnp.bfloat16), (lax.axis_size("col"),) + solved.shape)
    return lax.all_to_all(copies, "col", 0, 0, tiled=True)


def per_device(
    right_side,
    lower_inverse,
    lower_blocks,
    lower_pattern,
    upper_inverse,
    upper_blocks,
    upper_pattern,
):
    col_count = lax.axis_size("col")
    tiers = right_side.shape[0]
    right_rows = right_side[:, 0]
    low_inv = lower_inverse[:, 0]
    high_inv = upper_inverse[:, 0]
    low_blocks = lower_blocks[:, 0, :, 0]
    low_pattern = lower_pattern[:, 0, :, 0]
    high_blocks = upper_blocks[:, 0, :, 0]
    high_pattern = upper_pattern[:, 0, :, 0]
    block_shape = right_rows.shape[1:]
    history = jnp.zeros((tiers * col_count,) + block_shape, jnp.bfloat16)
    forward_list = []
    for tier_index in range(tiers):
        residual_now = right_rows[tier_index]
        if tier_index > 0:
            partial_value = level_terms(
                history, low_blocks[tier_index - 1], low_pattern[tier_index - 1]
            )
            residual_now = residual_now - reduce_rows(partial_value)
        solved = apply_inverse(low_inv[tier_index], residual_now)
        forward_list.append(solved)
        if tier_index < tiers - 1:
            history = history.at[tier_index * col_count : (tier_index + 1) * col_count].set(
                share_solved(solved)
            )
    history = jnp.zeros((tiers * col_count,) + block_shape, jnp.bfloat16)
    backward_list = [None] * tiers
    for tier_index in range(tiers - 1, -1, -1):
        residual_now = forward_list[tier_index]
        if tier_index < tiers - 1:
            partial_value = level_terms(history, high_blocks[tier_index], high_pattern[tier_index])
            residual_now = residual_now - reduce_rows(partial_value)
        solved = apply_inverse(high_inv[tier_index], residual_now)
        backward_list[tier_index] = solved
        if tier_index > 0:
            history = history.at[tier_index * col_count : (tier_index + 1) * col_count].set(
                share_solved(solved)
            )
    return (jnp.stack(forward_list)[:, None], jnp.stack(backward_list)[:, None])


def solution(mesh):
    in_specs = (
        P(None, ("col", "row"), None, None),
        P(None, ("col", "row"), None, None),
        P(None, "col", None, "row", None, None, None),
        P(None, "col", None, "row", None),
        P(None, ("col", "row"), None, None),
        P(None, "col", None, "row", None, None, None),
        P(None, "col", None, "row", None),
    )
    out_specs = (P(None, ("col", "row"), None, None), P(None, ("col", "row"), None, None))
    return jax.shard_map(
        per_device, mesh=mesh, in_specs=in_specs, out_specs=out_specs, check_vma=False
    )
```

```python
import functools

import jax
import jax.numpy as jnp
from jax import lax
from jax.experimental import pallas as pl
from jax.experimental.pallas import tpu as pltpu
from jax.sharding import PartitionSpec as P

BLOCKS_LAST = (((1,), (1,)), ((), ()))


def apply_inverse(inverse, vectors):
    return jnp.einsum("xi,oi->xo", vectors, inverse, precision=lax.Precision.HIGHEST)


def product_kernel(level, pattern_ref, history_ref, blocks_ref, sums_ref):
    rows, slots = blocks_ref.shape[1:3]
    for m in range(rows):
        total = None
        for s in range(slots):
            picked = history_ref[pattern_ref[(level * rows + m) * slots + s]]
            term = lax.dot_general(
                picked, blocks_ref[level, m, s], BLOCKS_LAST, preferred_element_type=jnp.float32
            )
            total = term if total is None else total + term
        sums_ref[m] = total.astype(sums_ref.dtype)


def level_terms(history, blocks, pattern, level):
    rows, slots, block = blocks.shape[1:4]
    vmem = pl.BlockSpec(memory_space=pltpu.VMEM)
    return pl.pallas_call(
        functools.partial(product_kernel, level),
        out_shape=jax.ShapeDtypeStruct((rows,) + history.shape[1:], jnp.bfloat16),
        in_specs=[pl.BlockSpec(memory_space=pltpu.SMEM), vmem, vmem],
        out_specs=vmem,
        compiler_params=pltpu.CompilerParams(vmem_limit_bytes=24 * 2**20),
        cost_estimate=pl.CostEstimate(
            flops=2 * rows * slots * history.shape[1] * block * block,
            bytes_accessed=2 * rows * slots * block * block + 2 * history.size,
            transcendentals=0,
        ),
    )(pattern.reshape(-1), history, blocks)


def reduce_rows(partial_value):
    parts = lax.all_to_all(partial_value, "row", 0, 0, tiled=True)
    return parts.astype(jnp.float32).sum(axis=0)


def share_solved(solved):
    copies = jnp.broadcast_to(solved.astype(jnp.bfloat16), (lax.axis_size("col"),) + solved.shape)
    return lax.all_to_all(copies, "col", 0, 0, tiled=True)


def per_device(
    right_side,
    lower_inverse,
    lower_blocks,
    lower_pattern,
    upper_inverse,
    upper_blocks,
    upper_pattern,
):
    col_count = lax.axis_size("col")
    tiers = right_side.shape[0]
    right_rows = right_side[:, 0]
    low_inv = lower_inverse[:, 0]
    high_inv = upper_inverse[:, 0]
    low_blocks = lower_blocks[:, 0, :, 0]
    low_pattern = lower_pattern[:, 0, :, 0]
    high_blocks = upper_blocks[:, 0, :, 0]
    high_pattern = upper_pattern[:, 0, :, 0]
    block_shape = right_rows.shape[1:]
    history = jnp.zeros((tiers * col_count,) + block_shape, jnp.bfloat16)
    forward_list = []
    for tier_index in range(tiers):
        residual_now = right_rows[tier_index]
        if tier_index > 0:
            partial_value = level_terms(history, low_blocks, low_pattern, tier_index - 1)
            residual_now = residual_now - reduce_rows(partial_value)
        solved = apply_inverse(low_inv[tier_index], residual_now)
        forward_list.append(solved)
        if tier_index < tiers - 1:
            history = history.at[tier_index * col_count : (tier_index + 1) * col_count].set(
                share_solved(solved)
            )
    history = jnp.zeros((tiers * col_count,) + block_shape, jnp.bfloat16)
    backward_list = [None] * tiers
    for tier_index in range(tiers - 1, -1, -1):
        residual_now = forward_list[tier_index]
        if tier_index < tiers - 1:
            partial_value = level_terms(history, high_blocks, high_pattern, tier_index)
            residual_now = residual_now - reduce_rows(partial_value)
        solved = apply_inverse(high_inv[tier_index], residual_now)
        backward_list[tier_index] = solved
        if tier_index > 0:
            history = history.at[tier_index * col_count : (tier_index + 1) * col_count].set(
                share_solved(solved)
            )
    return (jnp.stack(forward_list)[:, None], jnp.stack(backward_list)[:, None])


def solution(mesh):
    in_specs = (
        P(None, ("col", "row"), None, None),
        P(None, ("col", "row"), None, None),
        P(None, "col", None, "row", None, None, None),
        P(None, "col", None, "row", None),
        P(None, ("col", "row"), None, None),
        P(None, "col", None, "row", None, None, None),
        P(None, "col", None, "row", None),
    )
    out_specs = (P(None, ("col", "row"), None, None), P(None, ("col", "row"), None, None))
    return jax.shard_map(
        per_device, mesh=mesh, in_specs=in_specs, out_specs=out_specs, check_vma=False
    )
```

```python
import functools

import jax
import jax.numpy as jnp
from jax import lax
from jax.experimental import pallas as pl
from jax.experimental.pallas import tpu as pltpu
from jax.sharding import PartitionSpec as P

BLOCKS_LAST = (((1,), (1,)), ((), ()))
AXES = ("col", "row")
PARTIAL_TYPE = jnp.bfloat16
VLIM = 12
SLIM = 28


def apply_inverse(inverse, vectors):
    return jnp.einsum("xi,oi->xo", vectors, inverse, precision=lax.Precision.HIGHEST)


def product_kernel(level, index_ref, history_ref, even_ref, odd_ref, *sum_refs):
    rows, slots = odd_ref.shape[:2]
    patterns = (index_ref.shape[0] - 2) // 2

    @pl.when(index_ref[1] == 1)
    def _():
        for step, sums_ref in enumerate(sum_refs):
            chip = index_ref[0] ^ step
            for core in range(2):
                m = chip * 2 + core
                picked, taken = [], []
                for side, blocks_ref in enumerate((even_ref, odd_ref)):
                    for s in range(slots):
                        where = index_ref[2 + side * patterns + (level * rows + m) * slots + s]
                        picked.append(history_ref[where, side])
                        taken.append(blocks_ref[m, s])
                total = lax.dot_general(
                    jnp.concatenate(taken, 1),
                    jnp.concatenate(picked, 1),
                    BLOCKS_LAST,
                    preferred_element_type=jnp.float32,
                )
                sums_ref[core] = total.T.astype(sums_ref.dtype)

    @pl.when(index_ref[1] == 0)
    def _():
        for ref in sum_refs:
            ref[...] = jnp.zeros_like(ref)


def level_terms(index, history, blocks, level):
    rows, slots, block = blocks[1].shape[:3]
    steps = rows // 2
    vmem = pl.BlockSpec(memory_space=pltpu.VMEM)
    shape = (2,) + history.shape[2:]
    out_shape = [jax.ShapeDtypeStruct(shape, jnp.float32)]
    out_shape += [jax.ShapeDtypeStruct(shape, PARTIAL_TYPE)] * (steps - 1)
    return pl.pallas_call(
        functools.partial(product_kernel, level),
        out_shape=out_shape,
        in_specs=[pl.BlockSpec(memory_space=pltpu.SMEM)] + [vmem] * 3,
        out_specs=[vmem] * steps,
        compiler_params=pltpu.CompilerParams(vmem_limit_bytes=VLIM * 2**20),
        cost_estimate=pl.CostEstimate(
            flops=4 * rows * slots * history.shape[2] * block * block,
            bytes_accessed=4 * rows * slots * block * block + 2 * history.size,
            transcendentals=0,
        ),
    )(index, history, *blocks)


def stage_kernel(places, _, *refs):
    sources, held, arrived = refs[: len(places)], refs[len(places) : -1], refs[-1]
    copies = []
    for source, at, kept in zip(sources, places, held):
        if len(kept.shape) == 4:
            pieces = [(source.at[at, m], kept.at[m]) for m in range(kept.shape[0])]
        else:
            pieces = [(source.at[at], kept)]
        for piece in pieces:
            copies.append(pltpu.make_async_copy(*piece, arrived.at[len(copies)]))
    for copy in copies:
        copy.start()
    for copy in copies:
        copy.wait()


def stage(after, following):
    arrays, places = zip(*following)
    vmem = pl.BlockSpec(memory_space=pltpu.VMEM)
    hbm = pl.BlockSpec(memory_space=pltpu.HBM)
    out_shape = [jax.ShapeDtypeStruct(array.shape[1:], array.dtype) for array in arrays]
    pieces = sum(array.shape[1] if array.ndim == 5 else 1 for array in arrays)
    return pl.pallas_call(
        functools.partial(stage_kernel, places),
        out_shape=out_shape,
        in_specs=[vmem] + [hbm] * len(arrays),
        out_specs=[vmem] * len(out_shape),
        scratch_shapes=[pltpu.SemaphoreType.DMA((pieces,))],
        compiler_params=pltpu.CompilerParams(vmem_limit_bytes=SLIM * 2**20),
        cost_estimate=pl.CostEstimate(flops=0, bytes_accessed=3 * 2**20, transcendentals=0),
    )(after, *[pltpu.with_memory_space_constraint(array, pltpu.HBM) for array in arrays])


def stack_kernel(*refs):
    values, (even_ref, odd_ref) = refs[:-2], refs[-2:]
    turns, tiers = even_ref.shape[:2]
    for i in range(turns):
        for j in range(tiers):
            even_ref[i, j] = values[2 * (i * tiers + j)][...]
            odd_ref[i, j] = values[2 * (i * tiers + j) + 1][...]


def stack_levels(*turns):
    values = [value for levels in turns for pair in levels for value in pair]
    shape = jax.ShapeDtypeStruct((len(turns), len(turns[0])) + values[0].shape, values[0].dtype)
    vmem = pl.BlockSpec(memory_space=pltpu.VMEM)
    return pl.pallas_call(
        stack_kernel,
        out_shape=[shape, shape],
        in_specs=[vmem] * len(values),
        out_specs=[vmem, vmem],
    )(*values)


def swap_cores(value):
    count = lax.axis_size("row")
    return lax.ppermute(value, "row", [(i, i ^ 1) for i in range(count)])


def reduce_rows(parts):
    count = lax.axis_size("row")
    total = parts[0]
    for step in (2, 3, 1):
        pairs = [(i, i ^ (2 * step if i % 2 else 2)) for i in range(count)]
        total = total + lax.ppermute(parts[step], "row", pairs).astype(jnp.float32)
    return total


def gather_groups(col_count, row_count):
    side = 1
    while side * side < col_count:
        side *= 2
    at = lambda x, y, r: (x * side + y) * row_count + r
    groups = [
        [at(x, y, r) for x in range(side) for y in range(side)] for r in range(1, row_count, 2)
    ]
    for x in range(0, side, 2):
        for y in range(0, side, 2):
            groups.append(
                [at(x + i, y + j, r) for i in range(2) for j in range(2) for r in range(0, row_count, 2)]
            )
    return groups


def share_solved(even, odd):
    col_count, row_count = lax.axis_size("col"), lax.axis_size("row")
    pair = jnp.stack([even, odd]).astype(jnp.bfloat16)
    copies = jnp.broadcast_to(pair, (col_count,) + pair.shape)
    return lax.all_to_all(
        copies, AXES, 0, 0, tiled=True, axis_index_groups=gather_groups(col_count, row_count)
    )


def per_device(
    right_side,
    lower_inverse,
    lower_blocks,
    lower_pattern,
    upper_inverse,
    upper_blocks,
    upper_pattern,
):
    col_count = lax.axis_size("col")
    tiers = right_side.shape[0]
    place = lax.axis_index("row")
    is_odd = place % 2 == 1
    right_odd = right_side[:, 0]
    low_inv_odd = lower_inverse[:, 0]
    high_inv_odd = upper_inverse[:, 0]
    low_odd = lower_blocks[:, 0, :, 0]
    high_odd = upper_blocks[:, 0, :, 0]
    low_pattern = lower_pattern.reshape(-1)
    high_pattern = upper_pattern.reshape(-1)

    first_odd = apply_inverse(low_inv_odd[0], right_odd[0])
    first_even = swap_cores(first_odd)
    pattern_even = swap_cores(jnp.concatenate([low_pattern, high_pattern]))
    here = jnp.stack([place // 2, place % 2]).astype(jnp.int32)
    low_index = jnp.concatenate([here, pattern_even[: low_pattern.size], low_pattern])
    high_index = jnp.concatenate([here, pattern_even[low_pattern.size :], high_pattern])
    history = jnp.zeros((tiers * col_count, 2) + right_odd.shape[1:], jnp.bfloat16)
    first_even, start, right, low_inv, low, high_inv, high, history = lax.optimization_barrier(
        (first_even, low_odd[0], right_odd, low_inv_odd, low_odd, high_inv_odd, high_odd, history)
    )
    blocks = (swap_cores(start), start)
    right_even = swap_cores(right)
    low_inv_even = swap_cores(low_inv)
    low_even = swap_cores(low)
    high_inv_even = swap_cores(high_inv)
    high_even = swap_cores(high)

    forward = [(first_even, first_odd)]
    history = history.at[:col_count].set(share_solved(first_even, first_odd))
    for tier in range(1, tiers):
        following = [(low_inv_even, tier), (low_inv_odd, tier), (right_even, tier), (right_odd, tier)]
        if tier < tiers - 1:
            following += [(low_even, tier), (low_odd, tier)]
        else:
            following += [(high_even, tier - 1), (high_odd, tier - 1)]
            following += [(high_inv_even, tier), (high_inv_odd, tier)]
        parts = level_terms(low_index, history, blocks, tier - 1)
        kept = stage(parts[0], following)
        blocks, top_inv = kept[4:6], kept[6:]
        sums = reduce_rows(parts)
        even = apply_inverse(kept[0], kept[2] - sums[0])
        odd = apply_inverse(kept[1], kept[3] - sums[1])
        even, odd = lax.optimization_barrier((even, odd))
        forward.append((even, odd))
        if tier < tiers - 1:
            history = history.at[tier * col_count : (tier + 1) * col_count].set(
                share_solved(even, odd)
            )
    backward = [None] * tiers
    for tier in range(tiers - 1, -1, -1):
        even, odd = forward[tier]
        if tier < tiers - 1:
            following = [(high_inv_even, tier), (high_inv_odd, tier)]
            if tier > 0:
                following += [(high_even, tier - 1), (high_odd, tier - 1)]
            parts = level_terms(high_index, history, blocks, tier)
            kept = stage(parts[0], following)
            top_inv, blocks = kept[:2], kept[2:]
            sums = reduce_rows(parts)
            even, odd = even - sums[0], odd - sums[1]
        even = apply_inverse(top_inv[0], even)
        odd = apply_inverse(top_inv[1], odd)
        even, odd = lax.optimization_barrier((even, odd))
        backward[tier] = (even, odd)
        if tier > 0:
            history = history.at[tier * col_count : (tier + 1) * col_count].set(
                share_solved(even, odd)
            )
    evens, odds = stack_levels(forward, backward)
    evens = swap_cores(evens)
    outs = [jnp.where(is_odd, odds[i], evens[i]) for i in range(2)]
    return outs[0][:, None], outs[1][:, None]


def solution(mesh):
    in_specs = (
        P(None, ("col", "row"), None, None),
        P(None, ("col", "row"), None, None),
        P(None, "col", None, "row", None, None, None),
        P(None, "col", None, "row", None),
        P(None, ("col", "row"), None, None),
        P(None, "col", None, "row", None, None, None),
        P(None, "col", None, "row", None),
    )
    out_specs = (P(None, ("col", "row"), None, None), P(None, ("col", "row"), None, None))
    return jax.shard_map(
        per_device, mesh=mesh, in_specs=in_specs, out_specs=out_specs, check_vma=False
    )
```

```python
import functools

import jax
import jax.numpy as jnp
from jax import lax
from jax.experimental import pallas as pl
from jax.experimental.pallas import tpu as pltpu
from jax.sharding import PartitionSpec as P

BLOCKS_LAST = (((1,), (1,)), ((), ()))
AXES = ("col", "row")
PARTIAL_TYPE = jnp.bfloat16
VLIM = 12
SLIM = 12
TURN = 2


def apply_inverse(inverse, vectors):
    return jnp.einsum("xi,oi->xo", vectors, inverse, precision=lax.Precision.HIGHEST)


def product_kernel(level, index_ref, history_ref, even_ref, odd_ref, *sum_refs):
    rows, slots = odd_ref.shape[:2]
    patterns = (index_ref.shape[0] - 2) // 2

    @pl.when(index_ref[1] == 1)
    def _():
        for step, sums_ref in enumerate(sum_refs):
            chip = index_ref[0] ^ step
            for core in range(2):
                m = chip * 2 + core
                picked, taken = [], []
                for side, blocks_ref in enumerate((even_ref, odd_ref)):
                    for s in range(slots):
                        where = index_ref[2 + side * patterns + (level * rows + m) * slots + s]
                        picked.append(history_ref[where, side])
                        taken.append(blocks_ref[m, s])
                total = lax.dot_general(
                    jnp.concatenate(taken, 1),
                    jnp.concatenate(picked, 1),
                    BLOCKS_LAST,
                    preferred_element_type=jnp.float32,
                )
                sums_ref[core] = total.T.astype(sums_ref.dtype)

    @pl.when(index_ref[1] == 0)
    def _():
        for ref in sum_refs:
            ref[...] = jnp.zeros_like(ref)


def level_terms(index, history, blocks, level):
    rows, slots, block = blocks[1].shape[:3]
    steps = rows // 2
    vmem = pl.BlockSpec(memory_space=pltpu.VMEM)
    shape = (2,) + history.shape[2:]
    out_shape = [jax.ShapeDtypeStruct(shape, jnp.float32)]
    out_shape += [jax.ShapeDtypeStruct(shape, PARTIAL_TYPE)] * (steps - 1)
    return pl.pallas_call(
        functools.partial(product_kernel, level),
        out_shape=out_shape,
        in_specs=[pl.BlockSpec(memory_space=pltpu.SMEM)] + [vmem] * 3,
        out_specs=[vmem] * steps,
        compiler_params=pltpu.CompilerParams(vmem_limit_bytes=VLIM * 2**20),
        cost_estimate=pl.CostEstimate(
            flops=4 * rows * slots * history.shape[2] * block * block,
            bytes_accessed=4 * rows * slots * block * block + 2 * history.size,
            transcendentals=0,
        ),
    )(index, history, *blocks)


def stage_kernel(places, _, *refs):
    sources, held, arrived = refs[: len(places)], refs[len(places) : -1], refs[-1]
    copies = []
    for source, at, kept in zip(sources, places, held):
        if len(kept.shape) == 4:
            pieces = [(source.at[at, m], kept.at[m]) for m in range(kept.shape[0])]
        else:
            pieces = [(source.at[at], kept)]
        for piece in pieces:
            copies.append(pltpu.make_async_copy(*piece, arrived.at[len(copies)]))
    for copy in copies:
        copy.start()
    for copy in copies:
        copy.wait()


def stage(after, following):
    arrays, places = zip(*following)
    vmem = pl.BlockSpec(memory_space=pltpu.VMEM)
    hbm = pl.BlockSpec(memory_space=pltpu.HBM)
    out_shape = [jax.ShapeDtypeStruct(array.shape[1:], array.dtype) for array in arrays]
    pieces = sum(array.shape[1] if array.ndim == 5 else 1 for array in arrays)
    return pl.pallas_call(
        functools.partial(stage_kernel, places),
        out_shape=out_shape,
        in_specs=[vmem] + [hbm] * len(arrays),
        out_specs=[vmem] * len(out_shape),
        scratch_shapes=[pltpu.SemaphoreType.DMA((pieces,))],
        compiler_params=pltpu.CompilerParams(vmem_limit_bytes=SLIM * 2**20),
        cost_estimate=pl.CostEstimate(flops=0, bytes_accessed=3 * 2**20, transcendentals=0),
    )(after, *[in_hbm(array) for array in arrays])


def stack_kernel(*refs):
    values, (even_ref, odd_ref) = refs[:-2], refs[-2:]
    turns, tiers = even_ref.shape[:2]
    for i in range(turns):
        for j in range(tiers):
            even_ref[i, j] = values[2 * (i * tiers + j)][...]
            odd_ref[i, j] = values[2 * (i * tiers + j) + 1][...]


def stack_levels(*turns):
    values = [value for levels in turns for pair in levels for value in pair]
    shape = jax.ShapeDtypeStruct((len(turns), len(turns[0])) + values[0].shape, values[0].dtype)
    vmem = pl.BlockSpec(memory_space=pltpu.VMEM)
    return pl.pallas_call(
        stack_kernel,
        out_shape=[shape, shape],
        in_specs=[vmem] * len(values),
        out_specs=[vmem, vmem],
    )(*values)


def in_hbm(value):
    return pltpu.with_memory_space_constraint(value, pltpu.HBM)


def swap_cores(value):
    count = lax.axis_size("row")
    return lax.ppermute(value, "row", [(i, i ^ 1) for i in range(count)])


def reduce_rows(parts):
    count = lax.axis_size("row")
    total = parts[0]
    for step in (2, 3, 1):
        pairs = [(i, i ^ (2 * step if i % 2 else 2)) for i in range(count)]
        total = total + lax.ppermute(parts[step], "row", pairs).astype(jnp.float32)
    return total


def gather_groups(col_count, row_count):
    side = 1
    while side * side < col_count:
        side *= 2
    at = lambda x, y, r: (x * side + y) * row_count + r
    groups = [
        [at(x, y, r) for x in range(side) for y in range(side)] for r in range(1, row_count, 2)
    ]
    for x in range(0, side, 2):
        for y in range(0, side, 2):
            groups.append(
                [at(x + i, y + j, r) for i in range(2) for j in range(2) for r in range(0, row_count, 2)]
            )
    return groups


def share_solved(even, odd):
    col_count, row_count = lax.axis_size("col"), lax.axis_size("row")
    pair = jnp.stack([even, odd]).astype(jnp.bfloat16)
    copies = jnp.broadcast_to(pair, (col_count,) + pair.shape)
    return lax.all_to_all(
        copies, AXES, 0, 0, tiled=True, axis_index_groups=gather_groups(col_count, row_count)
    )


def per_device(
    right_side,
    lower_inverse,
    lower_blocks,
    lower_pattern,
    upper_inverse,
    upper_blocks,
    upper_pattern,
):
    col_count = lax.axis_size("col")
    tiers = right_side.shape[0]
    place = lax.axis_index("row")
    is_odd = place % 2 == 1
    right_odd = right_side[:, 0]
    low_inv_odd = lower_inverse[:, 0]
    high_inv_odd = upper_inverse[:, 0]
    low_odd = lower_blocks[:, 0, :, 0]
    high_odd = upper_blocks[:, 0, :, 0]
    low_pattern = lower_pattern.reshape(-1)
    high_pattern = upper_pattern.reshape(-1)

    first_odd = apply_inverse(low_inv_odd[0], right_odd[0])
    first_even = swap_cores(first_odd)
    pattern_even = swap_cores(jnp.concatenate([low_pattern, high_pattern]))
    here = jnp.stack([place // 2, place % 2]).astype(jnp.int32)
    low_index = jnp.concatenate([here, pattern_even[: low_pattern.size], low_pattern])
    high_index = jnp.concatenate([here, pattern_even[low_pattern.size :], high_pattern])
    low_index, high_index = lax.optimization_barrier((low_index, high_index))
    history = jnp.zeros((tiers * col_count, 2) + right_odd.shape[1:], jnp.bfloat16)
    first_even, start, right, low_inv, low, high_inv, high, history = lax.optimization_barrier(
        (first_even, low_odd[0], right_odd, low_inv_odd, low_odd, high_inv_odd, high_odd, history)
    )
    blocks = (swap_cores(start), start)
    right_even = swap_cores(right)
    low_inv_even = swap_cores(low_inv)
    low_even = in_hbm(swap_cores(in_hbm(low)))

    forward = [(first_even, first_odd)]
    history = history.at[:col_count].set(share_solved(first_even, first_odd))
    for tier in range(1, tiers):
        following = [(low_inv_even, tier), (low_inv_odd, tier), (right_even, tier), (right_odd, tier)]
        if tier < tiers - 1:
            following += [(low_even, tier), (low_odd, tier)]
        else:
            following += [(high_even, tier - 1), (high_odd, tier - 1)]
            following += [(high_inv_even, tier), (high_inv_odd, tier)]
        parts = level_terms(low_index, history, blocks, tier - 1)
        kept = stage(parts[0], following)
        blocks, top_inv = kept[4:6], kept[6:]
        sums = reduce_rows(parts)
        even = apply_inverse(kept[0], kept[2] - sums[0])
        odd = apply_inverse(kept[1], kept[3] - sums[1])
        even, odd = lax.optimization_barrier((even, odd))
        if tier == TURN:
            even, odd, high, high_inv = lax.optimization_barrier((even, odd, high, high_inv))
            high_inv_even = swap_cores(high_inv)
            high_even = in_hbm(swap_cores(in_hbm(high)))
        if tier == TURN + 3:
            even, odd, high_even, high_inv_even = lax.optimization_barrier(
                (even, odd, high_even, high_inv_even)
            )
        forward.append((even, odd))
        if tier < tiers - 1:
            history = history.at[tier * col_count : (tier + 1) * col_count].set(
                share_solved(even, odd)
            )
    backward = [None] * tiers
    for tier in range(tiers - 1, -1, -1):
        even, odd = forward[tier]
        if tier < tiers - 1:
            following = [(high_inv_even, tier), (high_inv_odd, tier)]
            if tier > 0:
                following += [(high_even, tier - 1), (high_odd, tier - 1)]
            parts = level_terms(high_index, history, blocks, tier)
            kept = stage(parts[0], following)
            top_inv, blocks = kept[:2], kept[2:]
            sums = reduce_rows(parts)
            even, odd = even - sums[0], odd - sums[1]
        even = apply_inverse(top_inv[0], even)
        odd = apply_inverse(top_inv[1], odd)
        even, odd = lax.optimization_barrier((even, odd))
        backward[tier] = (even, odd)
        if tier > 0:
            history = history.at[tier * col_count : (tier + 1) * col_count].set(
                share_solved(even, odd)
            )
    evens, odds = stack_levels(forward, backward)
    evens = swap_cores(evens)
    outs = [jnp.where(is_odd, odds[i], evens[i]) for i in range(2)]
    return outs[0][:, None], outs[1][:, None]


def solution(mesh):
    in_specs = (
        P(None, ("col", "row"), None, None),
        P(None, ("col", "row"), None, None),
        P(None, "col", None, "row", None, None, None),
        P(None, "col", None, "row", None),
        P(None, ("col", "row"), None, None),
        P(None, "col", None, "row", None, None, None),
        P(None, "col", None, "row", None),
    )
    out_specs = (P(None, ("col", "row"), None, None), P(None, ("col", "row"), None, None))
    return jax.shard_map(
        per_device, mesh=mesh, in_specs=in_specs, out_specs=out_specs, check_vma=False
    )
```

```python
import functools

import jax
import jax.numpy as jnp
from jax import lax
from jax.experimental import pallas as pl
from jax.experimental.pallas import tpu as pltpu
from jax.sharding import PartitionSpec as P

BLOCKS_LAST = (((1,), (1,)), ((), ()))
AXES = ("col", "row")
PARTIAL_TYPE = jnp.bfloat16
VLIM = 12
SLIM = 12
TURN = 2


def apply_inverse(inverse, vectors):
    return jnp.einsum("xi,oi->xo", vectors, inverse, precision=lax.Precision.HIGHEST)


def product_kernel(level, index_ref, history_ref, even_ref, odd_ref, *sum_refs):
    rows, slots = odd_ref.shape[:2]
    patterns = (index_ref.shape[0] - 2) // 2

    @pl.when(index_ref[1] == 1)
    def _():
        for step, sums_ref in enumerate(sum_refs):
            chip = index_ref[0] ^ step
            for core in range(2):
                m = chip * 2 + core
                picked, taken = [], []
                for side, blocks_ref in enumerate((even_ref, odd_ref)):
                    for s in range(slots):
                        where = index_ref[2 + side * patterns + (level * rows + m) * slots + s]
                        picked.append(history_ref[where, side])
                        taken.append(blocks_ref[m, s])
                total = lax.dot_general(
                    jnp.concatenate(taken, 1),
                    jnp.concatenate(picked, 1),
                    BLOCKS_LAST,
                    preferred_element_type=jnp.float32,
                )
                sums_ref[core] = total.T.astype(sums_ref.dtype)

    @pl.when(index_ref[1] == 0)
    def _():
        for ref in sum_refs:
            ref[...] = jnp.zeros_like(ref)


def level_terms(index, history, blocks, level):
    rows, slots, block = blocks[1].shape[:3]
    steps = rows // 2
    vmem = pl.BlockSpec(memory_space=pltpu.VMEM)
    shape = (2,) + history.shape[2:]
    out_shape = [jax.ShapeDtypeStruct(shape, jnp.float32)]
    out_shape += [jax.ShapeDtypeStruct(shape, PARTIAL_TYPE)] * (steps - 1)
    return pl.pallas_call(
        functools.partial(product_kernel, level),
        out_shape=out_shape,
        in_specs=[pl.BlockSpec(memory_space=pltpu.SMEM)] + [vmem] * 3,
        out_specs=[vmem] * steps,
        compiler_params=pltpu.CompilerParams(vmem_limit_bytes=VLIM * 2**20),
        cost_estimate=pl.CostEstimate(
            flops=4 * rows * slots * history.shape[2] * block * block,
            bytes_accessed=4 * rows * slots * block * block + 2 * history.size,
            transcendentals=0,
        ),
    )(index, history, *blocks)


def stage_kernel(places, _, *refs):
    sources, held, arrived = refs[: len(places)], refs[len(places) : -1], refs[-1]
    copies = []
    for source, at, kept in zip(sources, places, held):
        if len(kept.shape) == 4:
            pieces = [(source.at[at, m], kept.at[m]) for m in range(kept.shape[0])]
        else:
            pieces = [(source.at[at], kept)]
        for piece in pieces:
            copies.append(pltpu.make_async_copy(*piece, arrived.at[len(copies)]))
    for copy in copies:
        copy.start()
    for copy in copies:
        copy.wait()


def stage(after, following):
    arrays, places = zip(*following)
    vmem = pl.BlockSpec(memory_space=pltpu.VMEM)
    anywhere = pl.BlockSpec(memory_space=pl.ANY)
    out_shape = [jax.ShapeDtypeStruct(array.shape[1:], array.dtype) for array in arrays]
    pieces = sum(array.shape[1] if array.ndim == 5 else 1 for array in arrays)
    return pl.pallas_call(
        functools.partial(stage_kernel, places),
        out_shape=out_shape,
        in_specs=[vmem] + [anywhere] * len(arrays),
        out_specs=[vmem] * len(out_shape),
        scratch_shapes=[pltpu.SemaphoreType.DMA((pieces,))],
        compiler_params=pltpu.CompilerParams(vmem_limit_bytes=SLIM * 2**20),
        cost_estimate=pl.CostEstimate(flops=0, bytes_accessed=3 * 2**20, transcendentals=0),
    )(after, *[in_hbm(array) if array.size > 2**18 else array for array in arrays])


def stack_kernel(_, *refs):
    values, (even_ref, odd_ref) = refs[:-2], refs[-2:]
    for i in range(even_ref.shape[0]):
        even_ref[i] = values[2 * i][...]
        odd_ref[i] = values[2 * i + 1][...]


def stack_levels(after, levels):
    values = [value for pair in levels for value in pair]
    shape = jax.ShapeDtypeStruct((len(levels),) + values[0].shape, values[0].dtype)
    vmem = pl.BlockSpec(memory_space=pltpu.VMEM)
    return pl.pallas_call(
        stack_kernel,
        out_shape=[shape, shape],
        in_specs=[vmem] * (1 + len(values)),
        out_specs=[vmem, vmem],
        compiler_params=pltpu.CompilerParams(vmem_limit_bytes=4 * 2**20),
        cost_estimate=pl.CostEstimate(flops=0, bytes_accessed=2**20, transcendentals=0),
    )(after, *values)


def finish_kernel(first, odd_core_ref, even_ref, odd_ref, *refs):
    out_ref = refs[-1]
    tail = out_ref.shape[0] if len(refs) == 1 else out_ref.shape[0] - 1

    def write(kept_ref, last_ref):
        out_ref[out_ref.shape[0] - tail :] = kept_ref[first : first + tail]
        if last_ref is not None:
            out_ref[0] = last_ref[...]

    last_even, last_odd = refs[:2] if len(refs) == 3 else (None, None)
    pl.when(odd_core_ref[0] == 1)(lambda: write(odd_ref, last_odd))
    pl.when(odd_core_ref[0] == 0)(lambda: write(even_ref, last_even))


def finish(odd_core, evens, odds, first, tiers, last=()):
    vmem = pl.BlockSpec(memory_space=pltpu.VMEM)
    return pl.pallas_call(
        functools.partial(finish_kernel, first),
        out_shape=jax.ShapeDtypeStruct((tiers,) + odds.shape[1:], odds.dtype),
        in_specs=[pl.BlockSpec(memory_space=pltpu.SMEM)] + [vmem] * (2 + len(last)),
        out_specs=vmem,
        compiler_params=pltpu.CompilerParams(vmem_limit_bytes=4 * 2**20),
    )(odd_core, evens, odds, *last)


def in_hbm(value):
    return pltpu.with_memory_space_constraint(value, pltpu.HBM)


def swap_cores(value):
    count = lax.axis_size("row")
    return lax.ppermute(value, "row", [(i, i ^ 1) for i in range(count)])


def reduce_rows(parts):
    count = lax.axis_size("row")
    total = parts[0]
    for step in (2, 3, 1):
        pairs = [(i, i ^ (2 * step if i % 2 else 2)) for i in range(count)]
        total = total + lax.ppermute(parts[step], "row", pairs).astype(jnp.float32)
    return total


def gather_groups(col_count, row_count):
    side = 1
    while side * side < col_count:
        side *= 2
    at = lambda x, y, r: (x * side + y) * row_count + r
    groups = [
        [at(x, y, r) for x in range(side) for y in range(side)] for r in range(1, row_count, 2)
    ]
    for x in range(0, side, 2):
        for y in range(0, side, 2):
            groups.append(
                [at(x + i, y + j, r) for i in range(2) for j in range(2) for r in range(0, row_count, 2)]
            )
    return groups


def share_solved(even, odd):
    col_count, row_count = lax.axis_size("col"), lax.axis_size("row")
    pair = jnp.stack([even, odd]).astype(jnp.bfloat16)
    copies = jnp.broadcast_to(pair, (col_count,) + pair.shape)
    return lax.all_to_all(
        copies, AXES, 0, 0, tiled=True, axis_index_groups=gather_groups(col_count, row_count)
    )


def per_device(
    right_side,
    lower_inverse,
    lower_blocks,
    lower_pattern,
    upper_inverse,
    upper_blocks,
    upper_pattern,
):
    col_count = lax.axis_size("col")
    tiers = right_side.shape[0]
    place = lax.axis_index("row")
    is_odd = place % 2 == 1
    right_odd = right_side[:, 0]
    low_inv_odd = lower_inverse[:, 0]
    high_inv_odd = upper_inverse[:, 0]
    low_odd = lower_blocks[:, 0, :, 0]
    high_odd = upper_blocks[:, 0, :, 0]
    low_pattern = lower_pattern.reshape(-1)
    high_pattern = upper_pattern.reshape(-1)

    first_odd = apply_inverse(low_inv_odd[0], right_odd[0])
    first_even = swap_cores(first_odd)
    pattern_even = swap_cores(jnp.concatenate([low_pattern, high_pattern]))
    here = jnp.stack([place // 2, place % 2]).astype(jnp.int32)
    low_index = jnp.concatenate([here, pattern_even[: low_pattern.size], low_pattern])
    high_index = jnp.concatenate([here, pattern_even[low_pattern.size :], high_pattern])
    low_index, high_index = lax.optimization_barrier((low_index, high_index))
    history = jnp.zeros((tiers * col_count, 2) + right_odd.shape[1:], jnp.bfloat16)
    first_even, start, right, low_inv, low, high_inv, high, history = lax.optimization_barrier(
        (first_even, low_odd[0], right_odd, low_inv_odd, low_odd, high_inv_odd, high_odd, history)
    )
    blocks = (swap_cores(start), start)
    right_even = swap_cores(right)
    low_inv_even = swap_cores(low_inv)
    low_even = in_hbm(swap_cores(in_hbm(low)))

    forward = [(first_even, first_odd)]
    history = history.at[:col_count].set(share_solved(first_even, first_odd))
    for tier in range(1, tiers):
        following = [(low_inv_even, tier), (low_inv_odd, tier), (right_even, tier), (right_odd, tier)]
        if tier < tiers - 1:
            following += [(low_even, tier), (low_odd, tier)]
        else:
            following += [(high_even, tier - 1), (high_odd, tier - 1)]
            following += [(high_inv_even, tier), (high_inv_odd, tier)]
        parts = level_terms(low_index, history, blocks, tier - 1)
        kept = stage(parts[0], following)
        blocks, top_inv = kept[4:6], kept[6:]
        sums = reduce_rows(parts)
        even = apply_inverse(kept[0], kept[2] - sums[0])
        odd = apply_inverse(kept[1], kept[3] - sums[1])
        even, odd = lax.optimization_barrier((even, odd))
        if tier == TURN:
            even, odd, high, high_inv = lax.optimization_barrier((even, odd, high, high_inv))
            high_inv_even = swap_cores(high_inv)
            high_even = in_hbm(swap_cores(in_hbm(high)))
        if tier == TURN + 3:
            even, odd, high_even, high_inv_even = lax.optimization_barrier(
                (even, odd, high_even, high_inv_even)
            )
        forward.append((even, odd))
        if tier < tiers - 1:
            history = history.at[tier * col_count : (tier + 1) * col_count].set(
                share_solved(even, odd)
            )
    backward = [None] * tiers
    for tier in range(tiers - 1, -1, -1):
        even, odd = forward[tier]
        if tier < tiers - 1:
            following = [(high_inv_even, tier), (high_inv_odd, tier)]
            if tier > 0:
                following += [(high_even, tier - 1), (high_odd, tier - 1)]
            else:
                following += [(even[None], 0), (odd[None], 0)]
            parts = level_terms(high_index, history, blocks, tier)
            kept = stage(parts[0], following)
            top_inv, blocks = kept[:2], kept[2:]
            if tier == 0:
                even, odd = kept[2:]
                evens, odds = stack_levels(kept[0], forward + backward[1:])
                evens = swap_cores(evens)
            sums = reduce_rows(parts)
            even, odd = even - sums[0], odd - sums[1]
        even = apply_inverse(top_inv[0], even)
        odd = apply_inverse(top_inv[1], odd)
        even, odd = lax.optimization_barrier((even, odd))
        backward[tier] = (even, odd)
        if tier > 0:
            history = history.at[tier * col_count : (tier + 1) * col_count].set(
                share_solved(even, odd)
            )
    last_even, last_odd = backward[0]
    forward_out = finish(here[1:], evens, odds, 0, tiers)
    backward_out = finish(
        here[1:], evens, odds, tiers, tiers, (swap_cores(last_even), last_odd)
    )
    return forward_out[:, None], backward_out[:, None]


def solution(mesh):
    in_specs = (
        P(None, ("col", "row"), None, None),
        P(None, ("col", "row"), None, None),
        P(None, "col", None, "row", None, None, None),
        P(None, "col", None, "row", None),
        P(None, ("col", "row"), None, None),
        P(None, "col", None, "row", None, None, None),
        P(None, "col", None, "row", None),
    )
    out_specs = (P(None, ("col", "row"), None, None), P(None, ("col", "row"), None, None))
    return jax.shard_map(
        per_device, mesh=mesh, in_specs=in_specs, out_specs=out_specs, check_vma=False
    )
```

```python
import functools

import jax
import jax.numpy as jnp
from jax import lax
from jax.experimental import pallas as pl
from jax.experimental.pallas import tpu as pltpu
from jax.sharding import PartitionSpec as P

BLOCKS_LAST = (((1,), (1,)), ((), ()))
AXES = ("col", "row")
PARTIAL_TYPE = jnp.bfloat16
VLIM = 12
SLIM = 12
TURN = 2


def apply_inverse(inverse, vectors):
    return jnp.einsum("xi,oi->xo", vectors, inverse, precision=lax.Precision.HIGH)


def product_kernel(level, index_ref, history_ref, even_ref, odd_ref, *sum_refs):
    rows, slots = odd_ref.shape[:2]
    patterns = (index_ref.shape[0] - 2) // 2

    @pl.when(index_ref[1] == 1)
    def _():
        for step, sums_ref in enumerate(sum_refs):
            chip = index_ref[0] ^ step
            for core in range(2):
                m = chip * 2 + core
                picked, taken = [], []
                for side, blocks_ref in enumerate((even_ref, odd_ref)):
                    for s in range(slots):
                        where = index_ref[2 + side * patterns + (level * rows + m) * slots + s]
                        picked.append(history_ref[where, side])
                        taken.append(blocks_ref[m, s])
                total = lax.dot_general(
                    jnp.concatenate(taken, 1),
                    jnp.concatenate(picked, 1),
                    BLOCKS_LAST,
                    preferred_element_type=jnp.float32,
                )
                sums_ref[core] = total.T.astype(sums_ref.dtype)

    @pl.when(index_ref[1] == 0)
    def _():
        for ref in sum_refs:
            ref[...] = jnp.zeros_like(ref)


def level_terms(index, history, blocks, level):
    rows, slots, block = blocks[1].shape[:3]
    steps = rows // 2
    vmem = pl.BlockSpec(memory_space=pltpu.VMEM)
    shape = (2,) + history.shape[2:]
    out_shape = [jax.ShapeDtypeStruct(shape, jnp.float32)]
    out_shape += [jax.ShapeDtypeStruct(shape, PARTIAL_TYPE)] * (steps - 1)
    return pl.pallas_call(
        functools.partial(product_kernel, level),
        out_shape=out_shape,
        in_specs=[pl.BlockSpec(memory_space=pltpu.SMEM)] + [vmem] * 3,
        out_specs=[vmem] * steps,
        compiler_params=pltpu.CompilerParams(vmem_limit_bytes=VLIM * 2**20),
        cost_estimate=pl.CostEstimate(
            flops=4 * rows * slots * history.shape[2] * block * block,
            bytes_accessed=4 * rows * slots * block * block + 2 * history.size,
            transcendentals=0,
        ),
    )(index, history, *blocks)


def stage_kernel(places, _, *refs):
    sources, held, arrived = refs[: len(places)], refs[len(places) : -1], refs[-1]
    copies = []
    for source, at, kept in zip(sources, places, held):
        if len(kept.shape) == 4:
            pieces = [
                (source.at[at, pl.ds(m, 4)], kept.at[pl.ds(m, 4)]) for m in range(0, kept.shape[0], 4)
            ]
        else:
            pieces = [(source.at[at], kept)]
        for piece in pieces:
            copies.append(pltpu.make_async_copy(*piece, arrived.at[len(copies)]))
    @pl.when(lax.axis_index("row") % 2 == 1)
    def _():
        for copy in copies:
            copy.start()
        for copy in copies:
            copy.wait()


def stage(after, following):
    arrays, places = zip(*following)
    vmem = pl.BlockSpec(memory_space=pltpu.VMEM)
    anywhere = pl.BlockSpec(memory_space=pl.ANY)
    out_shape = [jax.ShapeDtypeStruct(array.shape[1:], array.dtype) for array in arrays]
    pieces = sum(array.shape[1] // 4 if array.ndim == 5 else 1 for array in arrays)
    return pl.pallas_call(
        functools.partial(stage_kernel, places),
        out_shape=out_shape,
        in_specs=[vmem] + [anywhere] * len(arrays),
        out_specs=[vmem] * len(out_shape),
        scratch_shapes=[pltpu.SemaphoreType.DMA((pieces,))],
        compiler_params=pltpu.CompilerParams(vmem_limit_bytes=SLIM * 2**20),
        cost_estimate=pl.CostEstimate(flops=0, bytes_accessed=3 * 2**20, transcendentals=0),
    )(after, *[in_hbm(array) if array.size > 2**18 else array for array in arrays])


def stack_kernel(_, *refs):
    values, (even_ref, odd_ref) = refs[:-2], refs[-2:]
    for i in range(even_ref.shape[0]):
        even_ref[i] = values[2 * i][...]
        odd_ref[i] = values[2 * i + 1][...]


def stack_levels(after, levels):
    values = [value for pair in levels for value in pair]
    shape = jax.ShapeDtypeStruct((len(levels),) + values[0].shape, values[0].dtype)
    vmem = pl.BlockSpec(memory_space=pltpu.VMEM)
    return pl.pallas_call(
        stack_kernel,
        out_shape=[shape, shape],
        in_specs=[vmem] * (1 + len(values)),
        out_specs=[vmem, vmem],
        compiler_params=pltpu.CompilerParams(vmem_limit_bytes=4 * 2**20),
        cost_estimate=pl.CostEstimate(flops=0, bytes_accessed=2**20, transcendentals=0),
    )(after, *values)


def finish_kernel(first, odd_core_ref, even_ref, odd_ref, *refs):
    out_ref = refs[-1]
    tail = out_ref.shape[0] if len(refs) == 1 else out_ref.shape[0] - 1

    def write(kept_ref, last_ref):
        out_ref[out_ref.shape[0] - tail :] = kept_ref[first : first + tail]
        if last_ref is not None:
            out_ref[0] = last_ref[...]

    last_even, last_odd = refs[:2] if len(refs) == 3 else (None, None)
    pl.when(odd_core_ref[0] == 1)(lambda: write(odd_ref, last_odd))
    pl.when(odd_core_ref[0] == 0)(lambda: write(even_ref, last_even))


def finish(odd_core, evens, odds, first, tiers, last=()):
    vmem = pl.BlockSpec(memory_space=pltpu.VMEM)
    return pl.pallas_call(
        functools.partial(finish_kernel, first),
        out_shape=jax.ShapeDtypeStruct((tiers,) + odds.shape[1:], odds.dtype),
        in_specs=[pl.BlockSpec(memory_space=pltpu.SMEM)] + [vmem] * (2 + len(last)),
        out_specs=vmem,
        compiler_params=pltpu.CompilerParams(vmem_limit_bytes=4 * 2**20),
    )(odd_core, evens, odds, *last)


def in_hbm(value):
    return pltpu.with_memory_space_constraint(value, pltpu.HBM)


def swap_cores(value):
    count = lax.axis_size("row")
    return lax.ppermute(value, "row", [(i, i ^ 1) for i in range(count)])


def reduce_rows(parts):
    count = lax.axis_size("row")
    total = parts[0]
    for step in (3, 2, 1):
        pairs = [(i, i ^ (2 * step if i % 2 else 2)) for i in range(count)]
        total = total + lax.ppermute(parts[step], "row", pairs).astype(jnp.float32)
    return total


def gather_groups(col_count, row_count):
    side = 1
    while side * side < col_count:
        side *= 2
    at = lambda x, y, r: (x * side + y) * row_count + r
    groups = [
        [at(x, y, r) for x in range(side) for y in range(side)] for r in range(1, row_count, 2)
    ]
    for x in range(0, side, 2):
        for y in range(0, side, 2):
            groups.append(
                [at(x + i, y + j, r) for i in range(2) for j in range(2) for r in range(0, row_count, 2)]
            )
    return groups


def share_solved(even, odd):
    col_count, row_count = lax.axis_size("col"), lax.axis_size("row")
    pair = jnp.stack([even, odd]).astype(jnp.bfloat16)
    copies = jnp.broadcast_to(pair, (col_count,) + pair.shape)
    return lax.all_to_all(
        copies, AXES, 0, 0, tiled=True, axis_index_groups=gather_groups(col_count, row_count)
    )


def per_device(
    right_side,
    lower_inverse,
    lower_blocks,
    lower_pattern,
    upper_inverse,
    upper_blocks,
    upper_pattern,
):
    col_count = lax.axis_size("col")
    tiers = right_side.shape[0]
    place = lax.axis_index("row")
    is_odd = place % 2 == 1
    right_odd = right_side[:, 0]
    low_inv_odd = lower_inverse[:, 0]
    high_inv_odd = upper_inverse[:, 0]
    low_odd = lower_blocks[:, 0, :, 0]
    high_odd = upper_blocks[:, 0, :, 0]
    low_pattern = lower_pattern.reshape(-1)
    high_pattern = upper_pattern.reshape(-1)

    first_odd = apply_inverse(low_inv_odd[0], right_odd[0])
    first_even = swap_cores(first_odd)
    pattern_even = swap_cores(jnp.concatenate([low_pattern, high_pattern]))
    here = jnp.stack([place // 2, place % 2]).astype(jnp.int32)
    low_index = jnp.concatenate([here, pattern_even[: low_pattern.size], low_pattern])
    high_index = jnp.concatenate([here, pattern_even[low_pattern.size :], high_pattern])
    low_index, high_index = lax.optimization_barrier((low_index, high_index))
    history = jnp.zeros((tiers * col_count, 2) + right_odd.shape[1:], jnp.bfloat16)
    first_even, start, right, low_inv, low, high_inv, high, history = lax.optimization_barrier(
        (first_even, low_odd[0], right_odd, low_inv_odd, low_odd, high_inv_odd, high_odd, history)
    )
    blocks = (swap_cores(start), start)
    right_even = swap_cores(right)
    low_inv_even = swap_cores(low_inv)
    low_even = in_hbm(swap_cores(in_hbm(low)))

    forward = [(first_even, first_odd)]
    history = history.at[:col_count].set(share_solved(first_even, first_odd))
    for tier in range(1, tiers):
        following = [(low_inv_even, tier), (low_inv_odd, tier), (right_even, tier), (right_odd, tier)]
        if tier < tiers - 1:
            following += [(low_even, tier), (low_odd, tier)]
        else:
            following += [(high_even, tier - 1), (high_odd, tier - 1)]
            following += [(high_inv_even, tier), (high_inv_odd, tier)]
        parts = level_terms(low_index, history, blocks, tier - 1)
        kept = stage(parts[0], following)
        blocks, top_inv = kept[4:6], kept[6:]
        sums = reduce_rows(parts)
        even = apply_inverse(kept[0], kept[2] - sums[0])
        odd = apply_inverse(kept[1], kept[3] - sums[1])
        even, odd = lax.optimization_barrier((even, odd))
        if tier == TURN:
            even, odd, high, high_inv = lax.optimization_barrier((even, odd, high, high_inv))
            high_inv_even = swap_cores(high_inv)
            high_even = in_hbm(swap_cores(in_hbm(high)))
        if tier == TURN + 3:
            even, odd, high_even, high_inv_even = lax.optimization_barrier(
                (even, odd, high_even, high_inv_even)
            )
        forward.append((even, odd))
        if tier < tiers - 1:
            history = history.at[tier * col_count : (tier + 1) * col_count].set(
                share_solved(even, odd)
            )
    backward = [None] * tiers
    for tier in range(tiers - 1, -1, -1):
        even, odd = forward[tier]
        if tier < tiers - 1:
            following = [(high_inv_even, tier), (high_inv_odd, tier)]
            if tier > 0:
                following += [(high_even, tier - 1), (high_odd, tier - 1)]
            else:
                following += [(even[None], 0), (odd[None], 0)]
            parts = level_terms(high_index, history, blocks, tier)
            kept = stage(parts[0], following)
            top_inv, blocks = kept[:2], kept[2:]
            if tier == 0:
                even, odd = kept[2:]
                evens, odds = stack_levels(kept[0], forward + backward[1:])
                evens = swap_cores(evens)
            sums = reduce_rows(parts)
            even, odd = even - sums[0], odd - sums[1]
        even = apply_inverse(top_inv[0], even)
        odd = apply_inverse(top_inv[1], odd)
        even, odd = lax.optimization_barrier((even, odd))
        backward[tier] = (even, odd)
        if tier > 0:
            history = history.at[tier * col_count : (tier + 1) * col_count].set(
                share_solved(even, odd)
            )
    last_even, last_odd = backward[0]
    forward_out = finish(here[1:], evens, odds, 0, tiers)
    backward_out = finish(
        here[1:], evens, odds, tiers, tiers, (swap_cores(last_even), last_odd)
    )
    return forward_out[:, None], backward_out[:, None]


def solution(mesh):
    in_specs = (
        P(None, ("col", "row"), None, None),
        P(None, ("col", "row"), None, None),
        P(None, "col", None, "row", None, None, None),
        P(None, "col", None, "row", None),
        P(None, ("col", "row"), None, None),
        P(None, "col", None, "row", None, None, None),
        P(None, "col", None, "row", None),
    )
    out_specs = (P(None, ("col", "row"), None, None), P(None, ("col", "row"), None, None))
    return jax.shard_map(
        per_device, mesh=mesh, in_specs=in_specs, out_specs=out_specs, check_vma=False
    )
```

```python
import functools

import jax
import jax.numpy as jnp
from jax import lax
from jax.experimental import pallas as pl
from jax.experimental.pallas import tpu as pltpu
from jax.sharding import PartitionSpec as P

BLOCKS_LAST = (((1,), (1,)), ((), ()))
AXES = ("col", "row")
PARTIAL_TYPE = jnp.float32
VLIM = 12
SLIM = 12
TURN = 2


def apply_inverse(inverse, vectors):
    return jnp.einsum("xi,oi->xo", vectors, inverse, precision=lax.Precision.HIGH)


def product_kernel(level, index_ref, history_ref, even_ref, odd_ref, *sum_refs):
    rows, slots = odd_ref.shape[:2]
    patterns = (index_ref.shape[0] - 2) // 2

    @pl.when(index_ref[1] == 1)
    def _():
        for step, sums_ref in enumerate(sum_refs):
            chip = index_ref[0] ^ step
            for core in range(2):
                m = chip * 2 + core
                picked, taken = [], []
                for side, blocks_ref in enumerate((even_ref, odd_ref)):
                    for s in range(slots):
                        where = index_ref[2 + side * patterns + (level * rows + m) * slots + s]
                        picked.append(history_ref[where, side])
                        taken.append(blocks_ref[m, s])
                total = lax.dot_general(
                    jnp.concatenate(taken, 1),
                    jnp.concatenate(picked, 1),
                    BLOCKS_LAST,
                    preferred_element_type=jnp.float32,
                )
                sums_ref[core] = total.T.astype(sums_ref.dtype)

    @pl.when(index_ref[1] == 0)
    def _():
        for ref in sum_refs:
            ref[...] = jnp.zeros_like(ref)


def level_terms(index, history, blocks, level):
    rows, slots, block = blocks[1].shape[:3]
    steps = rows // 2
    vmem = pl.BlockSpec(memory_space=pltpu.VMEM)
    shape = (2,) + history.shape[2:]
    out_shape = [jax.ShapeDtypeStruct(shape, jnp.float32)]
    out_shape += [jax.ShapeDtypeStruct(shape, PARTIAL_TYPE)] * (steps - 1)
    return pl.pallas_call(
        functools.partial(product_kernel, level),
        out_shape=out_shape,
        in_specs=[pl.BlockSpec(memory_space=pltpu.SMEM)] + [vmem] * 3,
        out_specs=[vmem] * steps,
        compiler_params=pltpu.CompilerParams(vmem_limit_bytes=VLIM * 2**20),
        cost_estimate=pl.CostEstimate(
            flops=4 * rows * slots * history.shape[2] * block * block,
            bytes_accessed=4 * rows * slots * block * block + 2 * history.size,
            transcendentals=0,
        ),
    )(index, history, *blocks)


def stage_kernel(places, _, *refs):
    sources, held, arrived = refs[: len(places)], refs[len(places) : -1], refs[-1]
    copies = []
    for source, at, kept in zip(sources, places, held):
        if len(kept.shape) == 4:
            pieces = [
                (source.at[at, pl.ds(m, 4)], kept.at[pl.ds(m, 4)]) for m in range(0, kept.shape[0], 4)
            ]
        else:
            pieces = [(source.at[at], kept)]
        for piece in pieces:
            copies.append(pltpu.make_async_copy(*piece, arrived.at[len(copies)]))
    @pl.when(lax.axis_index("row") % 2 == 1)
    def _():
        for copy in copies:
            copy.start()
        for copy in copies:
            copy.wait()


def stage(after, following):
    arrays, places = zip(*following)
    vmem = pl.BlockSpec(memory_space=pltpu.VMEM)
    anywhere = pl.BlockSpec(memory_space=pl.ANY)
    out_shape = [jax.ShapeDtypeStruct(array.shape[1:], array.dtype) for array in arrays]
    pieces = sum(array.shape[1] // 4 if array.ndim == 5 else 1 for array in arrays)
    return pl.pallas_call(
        functools.partial(stage_kernel, places),
        out_shape=out_shape,
        in_specs=[vmem] + [anywhere] * len(arrays),
        out_specs=[vmem] * len(out_shape),
        scratch_shapes=[pltpu.SemaphoreType.DMA((pieces,))],
        compiler_params=pltpu.CompilerParams(vmem_limit_bytes=SLIM * 2**20),
        cost_estimate=pl.CostEstimate(flops=0, bytes_accessed=3 * 2**20, transcendentals=0),
    )(after, *[in_hbm(array) if array.size > 2**18 else array for array in arrays])


def stack_kernel(_, *refs):
    values, (even_ref, odd_ref) = refs[:-2], refs[-2:]
    for i in range(even_ref.shape[0]):
        even_ref[i] = values[2 * i][...]
        odd_ref[i] = values[2 * i + 1][...]


def stack_levels(after, levels):
    values = [value for pair in levels for value in pair]
    shape = jax.ShapeDtypeStruct((len(levels),) + values[0].shape, values[0].dtype)
    vmem = pl.BlockSpec(memory_space=pltpu.VMEM)
    return pl.pallas_call(
        stack_kernel,
        out_shape=[shape, shape],
        in_specs=[vmem] * (1 + len(values)),
        out_specs=[vmem, vmem],
        compiler_params=pltpu.CompilerParams(vmem_limit_bytes=4 * 2**20),
        cost_estimate=pl.CostEstimate(flops=0, bytes_accessed=2**20, transcendentals=0),
    )(after, *values)


def finish_kernel(first, odd_core_ref, even_ref, odd_ref, *refs):
    out_ref = refs[-1]
    tail = out_ref.shape[0] if len(refs) == 1 else out_ref.shape[0] - 1

    def write(kept_ref, last_ref):
        out_ref[out_ref.shape[0] - tail :] = kept_ref[first : first + tail]
        if last_ref is not None:
            out_ref[0] = last_ref[...]

    last_even, last_odd = refs[:2] if len(refs) == 3 else (None, None)
    pl.when(odd_core_ref[0] == 1)(lambda: write(odd_ref, last_odd))
    pl.when(odd_core_ref[0] == 0)(lambda: write(even_ref, last_even))


def finish(odd_core, evens, odds, first, tiers, last=()):
    vmem = pl.BlockSpec(memory_space=pltpu.VMEM)
    return pl.pallas_call(
        functools.partial(finish_kernel, first),
        out_shape=jax.ShapeDtypeStruct((tiers,) + odds.shape[1:], odds.dtype),
        in_specs=[pl.BlockSpec(memory_space=pltpu.SMEM)] + [vmem] * (2 + len(last)),
        out_specs=vmem,
        compiler_params=pltpu.CompilerParams(vmem_limit_bytes=4 * 2**20),
    )(odd_core, evens, odds, *last)


def in_hbm(value):
    return pltpu.with_memory_space_constraint(value, pltpu.HBM)


def swap_cores(value):
    count = lax.axis_size("row")
    return lax.ppermute(value, "row", [(i, i ^ 1) for i in range(count)])


def reduce_rows(parts):
    count = lax.axis_size("row")
    total = parts[0]
    for step in (3, 2, 1):
        pairs = [(i, i ^ (2 * step if i % 2 else 2)) for i in range(count)]
        total = total + lax.ppermute(parts[step], "row", pairs).astype(jnp.float32)
    return total


def gather_groups(col_count, row_count):
    side = 1
    while side * side < col_count:
        side *= 2
    at = lambda x, y, r: (x * side + y) * row_count + r
    groups = [
        [at(x, y, r) for x in range(side) for y in range(side)] for r in range(1, row_count, 2)
    ]
    for x in range(0, side, 2):
        for y in range(0, side, 2):
            groups.append(
                [at(x + i, y + j, r) for i in range(2) for j in range(2) for r in range(0, row_count, 2)]
            )
    return groups


def share_solved(even, odd):
    col_count, row_count = lax.axis_size("col"), lax.axis_size("row")
    pair = jnp.stack([even, odd]).astype(jnp.bfloat16)
    copies = jnp.broadcast_to(pair, (col_count,) + pair.shape)
    return lax.all_to_all(
        copies, AXES, 0, 0, tiled=True, axis_index_groups=gather_groups(col_count, row_count)
    )


def per_device(
    right_side,
    lower_inverse,
    lower_blocks,
    lower_pattern,
    upper_inverse,
    upper_blocks,
    upper_pattern,
):
    col_count = lax.axis_size("col")
    tiers = right_side.shape[0]
    place = lax.axis_index("row")
    is_odd = place % 2 == 1
    right_odd = right_side[:, 0]
    low_inv_odd = lower_inverse[:, 0]
    high_inv_odd = upper_inverse[:, 0]
    low_odd = lower_blocks[:, 0, :, 0]
    high_odd = upper_blocks[:, 0, :, 0]
    low_pattern = lower_pattern.reshape(-1)
    high_pattern = upper_pattern.reshape(-1)

    first_odd = apply_inverse(low_inv_odd[0], right_odd[0])
    first_even = swap_cores(first_odd)
    pattern_even = swap_cores(jnp.concatenate([low_pattern, high_pattern]))
    here = jnp.stack([place // 2, place % 2]).astype(jnp.int32)
    low_index = jnp.concatenate([here, pattern_even[: low_pattern.size], low_pattern])
    high_index = jnp.concatenate([here, pattern_even[low_pattern.size :], high_pattern])
    low_index, high_index = lax.optimization_barrier((low_index, high_index))
    history = jnp.zeros((tiers * col_count, 2) + right_odd.shape[1:], jnp.bfloat16)
    first_even, start, right, low_inv, low, high_inv, high, history = lax.optimization_barrier(
        (first_even, low_odd[0], right_odd, low_inv_odd, low_odd, high_inv_odd, high_odd, history)
    )
    blocks = (swap_cores(start), start)
    right_even = swap_cores(right)
    low_inv_even = swap_cores(low_inv)
    low_even = in_hbm(swap_cores(in_hbm(low)))

    forward = [(first_even, first_odd)]
    history = history.at[:col_count].set(share_solved(first_even, first_odd))
    for tier in range(1, tiers):
        following = [(low_inv_even, tier), (low_inv_odd, tier), (right_even, tier), (right_odd, tier)]
        if tier < tiers - 1:
            following += [(low_even, tier), (low_odd, tier)]
        else:
            following += [(high_even, tier - 1), (high_odd, tier - 1)]
            following += [(high_inv_even, tier), (high_inv_odd, tier)]
        parts = level_terms(low_index, history, blocks, tier - 1)
        kept = stage(parts[0], following)
        blocks, top_inv = kept[4:6], kept[6:]
        sums = reduce_rows(parts)
        even = apply_inverse(kept[0], kept[2] - sums[0])
        odd = apply_inverse(kept[1], kept[3] - sums[1])
        even, odd = lax.optimization_barrier((even, odd))
        if tier == TURN:
            even, odd, high, high_inv = lax.optimization_barrier((even, odd, high, high_inv))
            high_inv_even = swap_cores(high_inv)
            high_even = in_hbm(swap_cores(in_hbm(high)))
        if tier == TURN + 3:
            even, odd, high_even, high_inv_even = lax.optimization_barrier(
                (even, odd, high_even, high_inv_even)
            )
        forward.append((even, odd))
        if tier < tiers - 1:
            history = history.at[tier * col_count : (tier + 1) * col_count].set(
                share_solved(even, odd)
            )
    backward = [None] * tiers
    for tier in range(tiers - 1, -1, -1):
        even, odd = forward[tier]
        if tier < tiers - 1:
            following = [(high_inv_even, tier), (high_inv_odd, tier)]
            if tier > 0:
                following += [(high_even, tier - 1), (high_odd, tier - 1)]
            else:
                following += [(even[None], 0), (odd[None], 0)]
            parts = level_terms(high_index, history, blocks, tier)
            kept = stage(parts[0], following)
            top_inv, blocks = kept[:2], kept[2:]
            if tier == 0:
                even, odd = kept[2:]
                evens, odds = stack_levels(kept[0], forward + backward[1:])
                evens = swap_cores(evens)
            sums = reduce_rows(parts)
            even, odd = even - sums[0], odd - sums[1]
        even = apply_inverse(top_inv[0], even)
        odd = apply_inverse(top_inv[1], odd)
        even, odd = lax.optimization_barrier((even, odd))
        backward[tier] = (even, odd)
        if tier > 0:
            history = history.at[tier * col_count : (tier + 1) * col_count].set(
                share_solved(even, odd)
            )
    last_even, last_odd = backward[0]
    forward_out = finish(here[1:], evens, odds, 0, tiers)
    backward_out = finish(
        here[1:], evens, odds, tiers, tiers, (swap_cores(last_even), last_odd)
    )
    return forward_out[:, None], backward_out[:, None]


def solution(mesh):
    in_specs = (
        P(None, ("col", "row"), None, None),
        P(None, ("col", "row"), None, None),
        P(None, "col", None, "row", None, None, None),
        P(None, "col", None, "row", None),
        P(None, ("col", "row"), None, None),
        P(None, "col", None, "row", None, None, None),
        P(None, "col", None, "row", None),
    )
    out_specs = (P(None, ("col", "row"), None, None), P(None, ("col", "row"), None, None))
    return jax.shard_map(
        per_device, mesh=mesh, in_specs=in_specs, out_specs=out_specs, check_vma=False
    )
```
